32 devices in a mesh: grp: 2 (over x), wid: 4 (over y, core), hid: 4 (over z).
Axes of the slice: x: 2, y: 2, z: 4, core: 2. Of those that a mesh axis runs over, the one named last changes fastest.
Arguments:
- tokens: bfloat16 [1536, 6144], P(('grp', 'hid'), 'wid'), parts along dimension 0, may hold values from -6 to 6
- expert_ids: int32 [1536, 2], P('grp'), parts along dimension 0, may hold values from 0 to 3, all different within a row
- gate_probs: float32 [1536, 2], P('grp'), parts along dimension 0, may hold values from 0.1 to 0.9
- gate_weight: bfloat16 [4, 6144, 8192], P(None, 'wid', 'hid'), may hold values from -0.078125 to 0.078125
- up_weight: bfloat16 [4, 6144, 8192], P(None, 'wid', 'hid'), may hold values from -0.078125 to 0.078125
- down_weight: bfloat16 [4, 8192, 6144], P(None, 'hid', 'wid'), may hold values from -0.0625 to 0.0625
Outputs:
- mixed: bfloat16 [1536, 6144], P(('grp', 'hid'), 'wid'), parts along dimension 0
The draws below stay inside these ranges and needn't reach their ends.
There are 2 independent parts, one for each index of `grp`. The reference program is written for one: setup_inputs(seed, part) draws one part's arguments, and reference() takes and returns one part's arrays. A program takes and returns all parts, laid end to end along the dimension named above; an argument that names none is the same for every part. Nothing has to cross between parts.
Inputs may be any that keep to these rules, and one draw needn't show every extreme that they name: `expert_ids`: each row names 2 different experts; every expert is named by some row.
All inputs are finite; a program needn't handle non-finite values.
Results may differ from the reference program's by a relative error of at most 0.02.
Values may be sent and summed in bfloat16 or wider, within the bound.
A program may use at most 256 MiB of HBM per device.

```python
import jax
import jax.numpy as jnp
from jax import lax

D = 6144
FF = 8192
EXPERTS = 4
TOPK = 2
ROWS = 768
ASSIGN = 1536
N_WID = 4


def block_levels(key, shape, shards, low, top_value):
    def one(axis_at, parts):
        draws = jax.random.uniform(jax.random.fold_in(jax.random.fold_in(key, 6), axis_at), (parts,), jnp.float32, low / len(shards), top_value / len(shards))
        return jnp.repeat(jnp.exp(draws), shape[axis_at] // parts).reshape((-1,) + (1,) * (len(shape) - axis_at - 1))

    level = one(*shards[0])
    for cut in shards[1:]:
        level = level * one(*cut)
    return level


def distinct(key, rows, amount, top, lift):
    ranking = jax.random.permutation(jax.random.fold_in(key, 1), amount)
    favour = ranking
    for power in range(3):
        favour = favour * favour // amount
    favour = favour * lift // amount
    chance = jax.random.randint(jax.random.fold_in(key, 2), (rows, amount), 0, 4096) + favour
    holders = jax.random.permutation(jax.random.fold_in(key, 3), rows)[jnp.arange(amount) % rows]
    chance = jnp.where(jnp.arange(rows)[:, None] == holders[None, :], 1 << 14, chance)
    score = chance * amount + jnp.arange(amount)
    return lax.top_k(score.astype(jnp.int32), top)[1].astype(jnp.int32)


def bell_draw(own_key, extent, deviation, limit, shards=(), kind=jnp.bfloat16):
    values = deviation * jax.random.normal(own_key, extent, jnp.float32)
    if shards:
        values = values * block_levels(own_key, extent, shards, -0.22, 0.18)
    return jnp.clip(values, -limit, limit).astype(kind)


def setup_inputs(seed: int = 0, part: int = 0) -> dict:
    arg_keys = jax.random.split(jax.random.key(seed), 7)
    part_keys = jax.random.split(jax.random.fold_in(arg_keys[6], part), 7)
    tokens = bell_draw(part_keys[0], (ROWS, D), 1.0, 6.0, ((0, 4), (1, 4)))
    expert_ids = distinct(part_keys[1], ROWS, EXPERTS, TOPK, 8192)
    gate_probs = jnp.clip(jax.random.uniform(part_keys[2], (ROWS, TOPK), jnp.float32, 0.1, 0.9), 0.1, 0.9)
    gate_weight = bell_draw(arg_keys[3], (EXPERTS, D, FF), D ** -0.5, 0.078125, ((1, 4), (2, 4)))
    up_weight = bell_draw(arg_keys[4], (EXPERTS, D, FF), D ** -0.5, 0.078125, ((1, 4), (2, 4)))
    down_weight = bell_draw(arg_keys[5], (EXPERTS, FF, D), FF ** -0.5, 0.0625, ((1, 4), (2, 4)))
    return {"tokens": tokens, "expert_ids": expert_ids, "gate_probs": gate_probs, "gate_weight": gate_weight, "up_weight": up_weight, "down_weight": down_weight}


def reference(tokens, expert_ids, gate_probs, gate_weight, up_weight, down_weight):
    flat_ids = expert_ids.reshape(-1).astype(jnp.int32)
    sort_order = jnp.argsort(flat_ids, stable=True).astype(jnp.int32)
    counts = jnp.sum((flat_ids[:, None] == jnp.arange(EXPERTS, dtype=jnp.int32)[None, :]).astype(jnp.int32), axis=0).astype(jnp.int32)
    sorted_rows = jnp.take(tokens, sort_order // TOPK, axis=0)
    width_block = D // N_WID

    def add_block(index, carry):
        start = (index * width_block)
        left = lax.dynamic_slice_in_dim(sorted_rows, start, width_block, 1)
        gate_rows = lax.dynamic_slice_in_dim(gate_weight, start, width_block, 1)
        up_rows = lax.dynamic_slice_in_dim(up_weight, start, width_block, 1)
        gate_piece = lax.ragged_dot(left, gate_rows, counts, preferred_element_type=jnp.float32)
        up_piece = lax.ragged_dot(left, up_rows, counts, preferred_element_type=jnp.float32)
        gate_piece = lax.optimization_barrier(gate_piece.astype(jnp.bfloat16)).astype(jnp.float32)
        up_piece = lax.optimization_barrier(up_piece.astype(jnp.bfloat16)).astype(jnp.float32)
        return (carry[0] + gate_piece, carry[1] + up_piece)

    empty = jnp.zeros((ASSIGN, FF), jnp.float32)
    gate_pre, up_pre = lax.fori_loop(0, N_WID, add_block, (empty, empty))
    hidden = (jax.nn.silu(gate_pre) * up_pre).astype(jnp.bfloat16)
    expert_out = lax.ragged_dot(hidden, down_weight, counts, preferred_element_type=jnp.float32)
    inverse = jnp.zeros((ASSIGN,), jnp.int32).at[sort_order].set(jnp.arange(ASSIGN, dtype=jnp.int32))
    unsorted = jnp.take(expert_out, inverse, axis=0).reshape(ROWS, TOPK, D)
    mixed = jnp.sum(unsorted * gate_probs.astype(jnp.float32)[:, :, None], axis=1)
    return mixed.astype(jnp.bfloat16)
```

```python
import functools

import jax
import jax.numpy as jnp
from jax import lax
from jax.experimental import pallas as pl
from jax.experimental.pallas import tpu as pltpu
from jax.sharding import PartitionSpec as P

MESH = pl.DeviceIdType.MESH
TOP = 2
H_SLOTS = 4


def block_at(me, apart, count):
    if count & (count - 1):
        return lax.rem(me + apart, count)
    total, bit = 0, 1
    while bit < count:
        total = total + bit * (((me // bit) % 2 + (apart // bit) % 2) % 2)
        bit *= 2
    return total


def back_at(apart, count):
    return apart if count & (count - 1) == 0 else count - apart


def kernel(
    n_wid, n_hid, width,
    tok_ref, ids_ref, probs_ref, gate_hbm, up_hbm, down_hbm, out_ref,
    x_all, w_gate, w_up, w_down, pre, s1_send, s1_recv, mine, s2_send, s2_recv, hidden, spread, acc, out_send, out_recv,
    w_sem, d_sem, x_ssem, x_rsem, s1_ssem, s1_rsem, s2_ssem, s2_rsem, s3_ssem, s3_rsem, s4_ssem, s4_rsem, o_ssem, o_rsem,
):
    rows, depth = tok_ref.shape
    experts, units = gate_hbm.shape[0], gate_hbm.shape[2]
    half = width // 2
    cuts = units // width
    steps = n_hid * cuts
    early = max(cuts - 1, 1)
    pairs = TOP * rows
    n_y = n_wid // 2
    share = pairs // n_y
    tile = 512 if depth % 512 == 0 else depth

    wid = lax.axis_index("wid")
    hid = lax.axis_index("hid")
    core = wid % 2
    y = wid // 2
    other = y * 2 + (1 - core)

    def y_at(shift):
        return (y + shift) % n_y

    def place(step):
        rest = step - early
        later = n_hid - 1 - rest // cuts
        is_first = step < early
        is_last = step >= early + (n_hid - 1) * cuts
        apart = jnp.where(is_first | is_last, 0, later)
        cut = jnp.where(is_first, step, jnp.where(is_last, step - (steps - cuts), rest % cuts))
        return apart, cut

    def first_use(apart):
        return early + (n_hid - 1 - apart) * cuts

    def weights_copy(step, slot):
        columns = pl.ds(pl.multiple_of(place(step)[1] * width, width), width)
        return [
            pltpu.make_async_copy(gate_hbm.at[:, :, columns], w_gate.at[slot], w_sem.at[slot, 0]),
            pltpu.make_async_copy(up_hbm.at[:, :, columns], w_up.at[slot], w_sem.at[slot, 1]),
        ]

    def down_copy(step, slot):
        lines = pl.ds(pl.multiple_of(place(step)[1] * width, width), width)
        return [
            pltpu.make_async_copy(
                down_hbm.at[e, lines, :], w_down.at[slot, pl.ds(e * width, width), :], d_sem.at[slot, e]
            )
            for e in range(experts)
        ]

    def start_all(copies):
        for copy in copies:
            copy.start()

    def token_copy(apart):
        return pltpu.make_async_remote_copy(
            src_ref=tok_ref, dst_ref=x_all.at[back_at(apart, n_hid)],
            send_sem=x_ssem.at[apart - 1], recv_sem=x_rsem.at[back_at(apart, n_hid) - 1],
            device_id={"hid": block_at(hid, apart, n_hid)}, device_id_type=MESH,
        )

    def token_arrival(apart):
        return pltpu.make_async_remote_copy(
            src_ref=tok_ref, dst_ref=x_all.at[apart],
            send_sem=x_ssem.at[apart - 1], recv_sem=x_rsem.at[apart - 1],
            device_id={"hid": block_at(hid, apart, n_hid)}, device_id_type=MESH,
        )

    def out_copy(apart, landing):
        return pltpu.make_async_remote_copy(
            src_ref=out_send.at[apart - 1], dst_ref=out_recv.at[landing - 1],
            send_sem=o_ssem.at[apart - 1], recv_sem=o_rsem.at[landing - 1],
            device_id={"hid": block_at(hid, apart, n_hid)}, device_id_type=MESH,
        )

    def s1_copy(step):
        slot = step % 2
        return pltpu.make_async_remote_copy(
            src_ref=s1_send, dst_ref=s1_recv.at[slot], send_sem=s1_ssem, recv_sem=s1_rsem.at[slot],
            device_id={"wid": other}, device_id_type=MESH,
        )

    def s2_copy(step, shift):
        slot, to = step % 2, y_at(shift)
        return pltpu.make_async_remote_copy(
            src_ref=s2_send.at[:, pl.ds(pl.multiple_of(to * share, share), share), :],
            dst_ref=s2_recv.at[slot, shift - 1],
            send_sem=s2_ssem.at[shift - 1], recv_sem=s2_rsem.at[slot, shift - 1],
            device_id={"wid": to * 2 + core}, device_id_type=MESH,
        )

    def s3_copy(step, shift, owner):
        slot = step % H_SLOTS
        part = hidden.at[slot, core, pl.ds(pl.multiple_of(owner * share, share), share), :]
        return pltpu.make_async_remote_copy(
            src_ref=part, dst_ref=part,
            send_sem=s3_ssem.at[shift - 1], recv_sem=s3_rsem.at[slot, shift - 1],
            device_id={"wid": y_at(shift) * 2 + core}, device_id_type=MESH,
        )

    def s4_copy(step, which):
        slot = step % H_SLOTS
        part = hidden.at[slot, which]
        return pltpu.make_async_remote_copy(
            src_ref=part, dst_ref=part, send_sem=s4_ssem.at[step % 2], recv_sem=s4_rsem.at[slot],
            device_id={"wid": other}, device_id_type=MESH,
        )

    start_all(weights_copy(0, 0))
    barrier = pltpu.get_barrier_semaphore()
    pl.semaphore_signal(barrier, inc=1, device_id={"wid": other}, device_id_type=MESH)
    for shift in range(1, n_y):
        pl.semaphore_signal(barrier, inc=1, device_id={"wid": y_at(shift) * 2 + core}, device_id_type=MESH)
    for apart in range(1, n_hid):
        pl.semaphore_signal(barrier, inc=1, device_id={"hid": block_at(hid, apart, n_hid)}, device_id_type=MESH)
    pl.semaphore_wait(barrier, n_y + n_hid - 1)

    token_copy(n_hid - 1).start()
    x_all[0] = tok_ref[...]
    start_all(down_copy(0, 0))

    def stage_d(step):
        for shift in range(1, n_y):
            s3_copy(step, shift, y).wait_send()
            s3_copy(step, shift, y_at(n_y - shift)).wait_recv()
        s4_copy(step, core).start()

    def stage_c(step):
        slot = step % 2
        gate, up = mine[0], mine[1]
        for shift in range(1, n_y):
            s2_copy(step, shift).wait_send()
            s2_copy(step, shift).wait_recv()
        for shift in range(1, n_y):
            gate = gate + s2_recv[slot, shift - 1, 0].astype(jnp.float32)
            up = up + s2_recv[slot, shift - 1, 1].astype(jnp.float32)
        block = block_at(hid, place(step)[0], n_hid)
        factor = probs_ref[pl.ds(pl.multiple_of(block * pairs + y * share, share), share), :]
        value = gate / (1.0 + jnp.exp(-gate)) * up * factor
        hidden[step % H_SLOTS, core, pl.ds(pl.multiple_of(y * share, share), share), :] = value.astype(jnp.bfloat16)
        for shift in range(1, n_y):
            s3_copy(step, shift, y).start()

    def stage_b(step):
        slot = step % 2
        s1_copy(step).wait_send()
        s1_copy(step).wait_recv()
        columns = pl.ds(pl.multiple_of(core * half, half), half)
        own = pl.ds(pl.multiple_of(y * share, share), share)
        for which in range(2):
            s2_send[which] = (pre[which, :, columns] + s1_recv[slot, which].astype(jnp.float32)).astype(jnp.bfloat16)
            mine[which] = pre[which, own, columns] + s1_recv[slot, which, own, :].astype(jnp.float32)
        for shift in range(1, n_y):
            s2_copy(step, shift).start()

    def stage_a(step):
        slot = step % 2
        for copy in weights_copy(step, slot):
            copy.wait()
        apart, cut = place(step)
        block = block_at(hid, apart, n_hid)
        x = x_all[apart]
        base = pl.multiple_of(block * pairs, pairs)
        ids = [ids_ref[pl.ds(pl.multiple_of(base + k * rows, rows), rows), :] for k in range(TOP)]
        for which, weight in ((0, w_gate), (1, w_up)):
            for e in range(experts):
                value = jnp.dot(x, weight[slot, e], preferred_element_type=jnp.float32)
                for k in range(TOP):
                    lines = slice(k * rows, (k + 1) * rows)
                    if e == 0:
                        pre[which, lines, :] = value
                    else:
                        pre[which, lines, :] = jnp.where(ids[k] == e, value, pre[which, lines, :])
        columns = pl.ds(pl.multiple_of((1 - core) * half, half), half)
        for which in range(2):
            s1_send[which] = pre[which, :, columns].astype(jnp.bfloat16)
        s1_copy(step).start()

    def stage_e(step):
        slot = step % 2
        s4_copy(step, core).wait_send()
        s4_copy(step, 1 - core).wait_recv()

        @pl.when(step + 1 < steps)
        def _():
            start_all(down_copy(step + 1, (step + 1) % 2))

        apart, cut = place(step)
        block = block_at(hid, apart, n_hid)
        base = pl.multiple_of(block * pairs, pairs)
        ids = [ids_ref[pl.ds(pl.multiple_of(base + k * rows, rows), rows), :] for k in range(TOP)]
        for side in range(2):
            parts = [hidden[step % H_SLOTS, side, k * rows:(k + 1) * rows, :].astype(jnp.float32) for k in range(TOP)]
            for e in range(experts):
                chosen = jnp.where(ids[0] == e, parts[0], jnp.where(ids[1] == e, parts[1], 0.0))
                start = e * width + side * half
                spread[:, start:start + half] = chosen.astype(jnp.bfloat16)
        for copy in down_copy(step, slot):
            copy.wait()
        keep = jnp.where(apart == 0, 0, 1)

        @pl.when((step == 0) | ((apart > 0) & (cut == 0)))
        def _():
            acc[keep] = jnp.zeros(acc.shape[1:], jnp.float32)

        for start in range(0, depth, tile):
            acc[keep, :, start:start + tile] += jnp.dot(
                spread[...], w_down[slot, :, start:start + tile], preferred_element_type=jnp.float32
            )

        for far in range(1, n_hid):
            @pl.when((apart == far) & (cut == cuts - 1))
            def _():
                out_send[far - 1] = acc[1].astype(jnp.bfloat16)
                out_copy(far, back_at(far, n_hid)).start()

    def body(i, carry):
        def at(step, stage):
            @pl.when((step >= 0) & (step < steps))
            def _():
                stage(step)

        @pl.when(i + 1 < steps)
        def _():
            start_all(weights_copy(i + 1, (i + 1) % 2))

        for apart in range(1, n_hid):
            if apart < n_hid - 1:
                @pl.when(i == first_use(apart + 1) - 1)
                def _():
                    token_copy(apart).start()

            @pl.when(i == first_use(apart))
            def _():
                token_arrival(apart).wait_recv()

        at(i - 3, stage_d)
        at(i - 2, stage_c)
        at(i - 1, stage_b)
        at(i, stage_a)
        at(i - 4, stage_e)
        return carry

    lax.fori_loop(0, steps + 4, body, 0)

    total = acc[0]
    for apart in range(1, n_hid):
        token_copy(apart).wait_send()
        out_copy(apart, apart).wait_send()
        out_copy(apart, apart).wait_recv()
        total = total + out_recv[apart - 1].astype(jnp.float32)
    out_ref[...] = total.astype(jnp.bfloat16)


def shards(n_wid, n_hid, tokens, expert_ids, gate_probs, gate_weight, up_weight, down_weight):
    rows, depth = tokens.shape
    experts, _, units = gate_weight.shape
    width = 512
    half = width // 2
    n_y = n_wid // 2
    pairs = TOP * rows
    share = pairs // n_y
    ids = expert_ids.reshape(n_hid, rows, TOP).transpose(0, 2, 1).reshape(n_hid * pairs, 1)
    probs = gate_probs.reshape(n_hid, rows, TOP).transpose(0, 2, 1).reshape(n_hid * pairs, 1)
    vmem = pl.BlockSpec(memory_space=pltpu.VMEM)
    hbm = pl.BlockSpec(memory_space=pl.ANY)
    bf16, f32 = jnp.bfloat16, jnp.float32
    dma = pltpu.SemaphoreType.DMA
    work = 2 * n_hid * rows * experts * depth * units * 3
    return pl.pallas_call(
        functools.partial(kernel, n_wid, n_hid, width),
        out_shape=jax.ShapeDtypeStruct((rows, depth), bf16),
        in_specs=[vmem, vmem, vmem, hbm, hbm, hbm],
        out_specs=vmem,
        scratch_shapes=[
            pltpu.VMEM((n_hid, rows, depth), bf16),
            pltpu.VMEM((2, experts, depth, width), bf16),
            pltpu.VMEM((2, experts, depth, width), bf16),
            pltpu.VMEM((2, experts * width, depth), bf16),
            pltpu.VMEM((2, pairs, width), f32),
            pltpu.VMEM((2, pairs, half), bf16),
            pltpu.VMEM((2, 2, pairs, half), bf16),
            pltpu.VMEM((2, share, half), f32),
            pltpu.VMEM((2, pairs, half), bf16),
            pltpu.VMEM((2, n_y - 1, 2, share, half), bf16),
            pltpu.VMEM((H_SLOTS, 2, pairs, half), bf16),
            pltpu.VMEM((rows, experts * width), bf16),
            pltpu.VMEM((2, rows, depth), f32),
            pltpu.VMEM((n_hid - 1, rows, depth), bf16),
            pltpu.VMEM((n_hid - 1, rows, depth), bf16),
            dma((2, 2)),
            dma((2, experts)),
            dma((n_hid - 1,)),
            dma((n_hid - 1,)),
            dma,
            dma((2,)),
            dma((n_y - 1,)),
            dma((2, n_y - 1)),
            dma((n_y - 1,)),
            dma((H_SLOTS, n_y - 1)),
            dma((2,)),
            dma((H_SLOTS,)),
            dma((n_hid - 1,)),
            dma((n_hid - 1,)),
        ],
        compiler_params=pltpu.CompilerParams(
            collective_id=0, has_side_effects=True, vmem_limit_bytes=60 * 1024 * 1024
        ),
        cost_estimate=pl.CostEstimate(
            flops=work, bytes_accessed=n_hid * experts * depth * units * 6, transcendentals=0
        ),
        name="expert_layer",
    )(tokens, ids, probs, gate_weight, up_weight, down_weight)


def solution(mesh):
    in_specs = (
        P(("grp", "hid"), "wid"),
        P("grp", None),
        P("grp", None),
        P(None, "wid", "hid"),
        P(None, "wid", "hid"),
        P(None, "hid", "wid"),
    )
    out_specs = P(("grp", "hid"), "wid")
    return jax.shard_map(
        functools.partial(shards, mesh.shape["wid"], mesh.shape["hid"]),
        mesh=mesh, in_specs=in_specs, out_specs=out_specs, check_vma=False,
    )
```

```python
import functools

import jax
import jax.numpy as jnp
from jax import lax
from jax.experimental import pallas as pl
from jax.experimental.pallas import tpu as pltpu
from jax.sharding import PartitionSpec as P

MESH = pl.DeviceIdType.MESH
TOP = 2
H_SLOTS = 4


def block_at(me, apart, count):
    if count & (count - 1):
        return lax.rem(me + apart, count)
    total, bit = 0, 1
    while bit < count:
        total = total + bit * (((me // bit) % 2 + (apart // bit) % 2) % 2)
        bit *= 2
    return total


def back_at(apart, count):
    return apart if count & (count - 1) == 0 else count - apart


def kernel(
    n_wid, n_hid, width,
    tok_ref, ids_ref, probs_ref, gate_hbm, up_hbm, down_hbm, out_ref,
    x_all, w_gate, w_up, w_down, pre, s1_send, s1_recv, mine, s2_send, s2_recv, hidden, spread, acc, out_send, out_recv, factors,
    w_sem, d_sem, x_ssem, x_rsem, s1_ssem, s1_rsem, s2_ssem, s2_rsem, s3_ssem, s3_rsem, s4_ssem, s4_rsem, o_ssem, o_rsem,
):
    rows, depth = tok_ref.shape
    experts, units = gate_hbm.shape[0], gate_hbm.shape[2]
    half = width // 2
    cuts = units // width
    steps = n_hid * cuts
    early = max(cuts - 1, 1)
    pairs = TOP * rows
    n_y = n_wid // 2
    share = pairs // n_y
    tile = 512 if depth % 512 == 0 else depth

    wid = lax.axis_index("wid")
    hid = lax.axis_index("hid")
    core = wid % 2
    y = wid // 2
    other = y * 2 + (1 - core)

    def y_at(shift):
        return (y + shift) % n_y

    def place(step):
        rest = step - early
        later = n_hid - 1 - rest // cuts
        is_first = step < early
        is_last = step >= early + (n_hid - 1) * cuts
        apart = jnp.where(is_first | is_last, 0, later)
        cut = jnp.where(is_first, step, jnp.where(is_last, step - (steps - cuts), rest % cuts))
        return apart, cut

    def first_use(apart):
        return early + (n_hid - 1 - apart) * cuts

    def weights_copy(step, slot):
        columns = pl.ds(pl.multiple_of(place(step)[1] * width, width), width)
        return [
            pltpu.make_async_copy(gate_hbm.at[:, :, columns], w_gate.at[slot], w_sem.at[slot, 0]),
            pltpu.make_async_copy(up_hbm.at[:, :, columns], w_up.at[slot], w_sem.at[slot, 1]),
        ]

    def down_copy(step, slot):
        lines = pl.ds(pl.multiple_of(place(step)[1] * width, width), width)
        return [
            pltpu.make_async_copy(
                down_hbm.at[e, lines, :], w_down.at[slot, pl.ds(e * width, width), :], d_sem.at[slot, e]
            )
            for e in range(experts)
        ]

    def start_all(copies):
        for copy in copies:
            copy.start()

    def token_copy(apart):
        return pltpu.make_async_remote_copy(
            src_ref=tok_ref, dst_ref=x_all.at[back_at(apart, n_hid)],
            send_sem=x_ssem.at[apart - 1], recv_sem=x_rsem.at[back_at(apart, n_hid) - 1],
            device_id={"hid": block_at(hid, apart, n_hid)}, device_id_type=MESH,
        )

    def token_arrival(apart):
        return pltpu.make_async_remote_copy(
            src_ref=tok_ref, dst_ref=x_all.at[apart],
            send_sem=x_ssem.at[apart - 1], recv_sem=x_rsem.at[apart - 1],
            device_id={"hid": block_at(hid, apart, n_hid)}, device_id_type=MESH,
        )

    def out_copy(apart, landing):
        return pltpu.make_async_remote_copy(
            src_ref=out_send.at[apart - 1], dst_ref=out_recv.at[landing - 1],
            send_sem=o_ssem.at[apart - 1], recv_sem=o_rsem.at[landing - 1],
            device_id={"hid": block_at(hid, apart, n_hid)}, device_id_type=MESH,
        )

    def s1_copy(step):
        slot = step % 2
        return pltpu.make_async_remote_copy(
            src_ref=s1_send, dst_ref=s1_recv.at[slot], send_sem=s1_ssem, recv_sem=s1_rsem.at[slot],
            device_id={"wid": other}, device_id_type=MESH,
        )

    def s2_copy(step, shift):
        slot, to = step % 2, y_at(shift)
        return pltpu.make_async_remote_copy(
            src_ref=s2_send.at[:, pl.ds(pl.multiple_of(to * share, share), share), :],
            dst_ref=s2_recv.at[slot, shift - 1],
            send_sem=s2_ssem.at[shift - 1], recv_sem=s2_rsem.at[slot, shift - 1],
            device_id={"wid": to * 2 + core}, device_id_type=MESH,
        )

    def s3_copy(step, shift, owner):
        slot = step % H_SLOTS
        part = hidden.at[slot, core, pl.ds(pl.multiple_of(owner * share, share), share), :]
        return pltpu.make_async_remote_copy(
            src_ref=part, dst_ref=part,
            send_sem=s3_ssem.at[shift - 1], recv_sem=s3_rsem.at[slot, shift - 1],
            device_id={"wid": y_at(shift) * 2 + core}, device_id_type=MESH,
        )

    def s4_copy(step, which):
        slot = step % H_SLOTS
        part = hidden.at[slot, which]
        return pltpu.make_async_remote_copy(
            src_ref=part, dst_ref=part, send_sem=s4_ssem.at[step % 2], recv_sem=s4_rsem.at[slot],
            device_id={"wid": other}, device_id_type=MESH,
        )

    start_all(weights_copy(0, 0))
    barrier = pltpu.get_barrier_semaphore()
    pl.semaphore_signal(barrier, inc=1, device_id={"wid": other}, device_id_type=MESH)
    for shift in range(1, n_y):
        pl.semaphore_signal(barrier, inc=1, device_id={"wid": y_at(shift) * 2 + core}, device_id_type=MESH)
    for apart in range(1, n_hid):
        pl.semaphore_signal(barrier, inc=1, device_id={"hid": block_at(hid, apart, n_hid)}, device_id_type=MESH)
    pl.semaphore_wait(barrier, n_y + n_hid - 1)

    token_copy(n_hid - 1).start()
    x_all[0] = tok_ref[...]
    for block in range(n_hid):
        for k in range(TOP):
            start = block * pairs + k * rows
            factors[start:start + rows, :] = probs_ref[block * rows:(block + 1) * rows, k:k + 1]
    start_all(down_copy(0, 0))

    def stage_d(step):
        for shift in range(1, n_y):
            s3_copy(step, shift, y).wait_send()
            s3_copy(step, shift, y_at(n_y - shift)).wait_recv()
        s4_copy(step, core).start()

    def stage_c(step):
        slot = step % 2
        gate, up = mine[0], mine[1]
        for shift in range(1, n_y):
            s2_copy(step, shift).wait_send()
            s2_copy(step, shift).wait_recv()
        for shift in range(1, n_y):
            gate = gate + s2_recv[slot, shift - 1, 0].astype(jnp.float32)
            up = up + s2_recv[slot, shift - 1, 1].astype(jnp.float32)
        block = block_at(hid, place(step)[0], n_hid)
        factor = factors[pl.ds(pl.multiple_of(block * pairs + y * share, share), share), :]
        value = gate / (1.0 + jnp.exp(-gate)) * up * factor
        hidden[step % H_SLOTS, core, pl.ds(pl.multiple_of(y * share, share), share), :] = value.astype(jnp.bfloat16)
        for shift in range(1, n_y):
            s3_copy(step, shift, y).start()

    def stage_b(step):
        slot = step % 2
        s1_copy(step).wait_send()
        s1_copy(step).wait_recv()
        columns = pl.ds(pl.multiple_of(core * half, half), half)
        own = pl.ds(pl.multiple_of(y * share, share), share)
        for which in range(2):
            s2_send[which] = (pre[which, :, columns] + s1_recv[slot, which].astype(jnp.float32)).astype(jnp.bfloat16)
            mine[which] = pre[which, own, columns] + s1_recv[slot, which, own, :].astype(jnp.float32)
        for shift in range(1, n_y):
            s2_copy(step, shift).start()

    def stage_a(step):
        slot = step % 2
        for copy in weights_copy(step, slot):
            copy.wait()
        apart, cut = place(step)
        block = block_at(hid, apart, n_hid)
        x = x_all[apart]
        lines = pl.ds(pl.multiple_of(block * rows, rows), rows)
        ids = [ids_ref[lines, k:k + 1] for k in range(TOP)]
        for which, weight in ((0, w_gate), (1, w_up)):
            for e in range(experts):
                value = jnp.dot(x, weight[slot, e], preferred_element_type=jnp.float32)
                for k in range(TOP):
                    lines = slice(k * rows, (k + 1) * rows)
                    if e == 0:
                        pre[which, lines, :] = value
                    else:
                        pre[which, lines, :] = jnp.where(ids[k] == e, value, pre[which, lines, :])
        columns = pl.ds(pl.multiple_of((1 - core) * half, half), half)
        for which in range(2):
            s1_send[which] = pre[which, :, columns].astype(jnp.bfloat16)
        s1_copy(step).start()

    def stage_e(step):
        slot = step % 2
        s4_copy(step, core).wait_send()
        s4_copy(step, 1 - core).wait_recv()

        @pl.when(step + 1 < steps)
        def _():
            start_all(down_copy(step + 1, (step + 1) % 2))

        apart, cut = place(step)
        block = block_at(hid, apart, n_hid)
        lines = pl.ds(pl.multiple_of(block * rows, rows), rows)
        ids = [ids_ref[lines, k:k + 1] for k in range(TOP)]
        for side in range(2):
            parts = [hidden[step % H_SLOTS, side, k * rows:(k + 1) * rows, :].astype(jnp.float32) for k in range(TOP)]
            for e in range(experts):
                chosen = jnp.where(ids[0] == e, parts[0], jnp.where(ids[1] == e, parts[1], 0.0))
                start = e * width + side * half
                spread[:, start:start + half] = chosen.astype(jnp.bfloat16)
        for copy in down_copy(step, slot):
            copy.wait()
        keep = jnp.where(apart == 0, 0, 1)

        @pl.when((step == 0) | ((apart > 0) & (cut == 0)))
        def _():
            acc[keep] = jnp.zeros(acc.shape[1:], jnp.float32)

        for start in range(0, depth, tile):
            acc[keep, :, start:start + tile] += jnp.dot(
                spread[...], w_down[slot, :, start:start + tile], preferred_element_type=jnp.float32
            )

        for far in range(1, n_hid):
            @pl.when((apart == far) & (cut == cuts - 1))
            def _():
                out_send[far - 1] = acc[1].astype(jnp.bfloat16)
                out_copy(far, back_at(far, n_hid)).start()

    def body(i, carry):
        def at(step, stage):
            @pl.when((step >= 0) & (step < steps))
            def _():
                stage(step)

        @pl.when(i + 1 < steps)
        def _():
            start_all(weights_copy(i + 1, (i + 1) % 2))

        for apart in range(1, n_hid):
            if apart < n_hid - 1:
                @pl.when(i == first_use(apart + 1) - 1)
                def _():
                    token_copy(apart).start()

            @pl.when(i == first_use(apart))
            def _():
                token_arrival(apart).wait_recv()

        at(i - 3, stage_d)
        at(i - 2, stage_c)
        at(i - 1, stage_b)
        at(i, stage_a)
        at(i - 4, stage_e)
        return carry

    lax.fori_loop(0, steps + 4, body, 0)

    total = acc[0]
    for apart in range(1, n_hid):
        token_copy(apart).wait_send()
        out_copy(apart, apart).wait_send()
        out_copy(apart, apart).wait_recv()
        total = total + out_recv[apart - 1].astype(jnp.float32)
    out_ref[...] = total.astype(jnp.bfloat16)


def shards(n_wid, n_hid, tokens, expert_ids, gate_probs, gate_weight, up_weight, down_weight):
    rows, depth = tokens.shape
    experts, _, units = gate_weight.shape
    width = 512
    half = width // 2
    n_y = n_wid // 2
    pairs = TOP * rows
    share = pairs // n_y
    vmem = pl.BlockSpec(memory_space=pltpu.VMEM)
    hbm = pl.BlockSpec(memory_space=pl.ANY)
    bf16, f32 = jnp.bfloat16, jnp.float32
    dma = pltpu.SemaphoreType.DMA
    work = 2 * n_hid * rows * experts * depth * units * 3
    return pl.pallas_call(
        functools.partial(kernel, n_wid, n_hid, width),
        out_shape=jax.ShapeDtypeStruct((rows, depth), bf16),
        in_specs=[vmem, vmem, vmem, hbm, hbm, hbm],
        out_specs=vmem,
        scratch_shapes=[
            pltpu.VMEM((n_hid, rows, depth), bf16),
            pltpu.VMEM((2, experts, depth, width), bf16),
            pltpu.VMEM((2, experts, depth, width), bf16),
            pltpu.VMEM((2, experts * width, depth), bf16),
            pltpu.VMEM((2, pairs, width), f32),
            pltpu.VMEM((2, pairs, half), bf16),
            pltpu.VMEM((2, 2, pairs, half), bf16),
            pltpu.VMEM((2, share, half), f32),
            pltpu.VMEM((2, pairs, half), bf16),
            pltpu.VMEM((2, n_y - 1, 2, share, half), bf16),
            pltpu.VMEM((H_SLOTS, 2, pairs, half), bf16),
            pltpu.VMEM((rows, experts * width), bf16),
            pltpu.VMEM((2, rows, depth), f32),
            pltpu.VMEM((n_hid - 1, rows, depth), bf16),
            pltpu.VMEM((n_hid - 1, rows, depth), bf16),
            pltpu.VMEM((n_hid * pairs, 1), f32),
            dma((2, 2)),
            dma((2, experts)),
            dma((n_hid - 1,)),
            dma((n_hid - 1,)),
            dma,
            dma((2,)),
            dma((n_y - 1,)),
            dma((2, n_y - 1)),
            dma((n_y - 1,)),
            dma((H_SLOTS, n_y - 1)),
            dma((2,)),
            dma((H_SLOTS,)),
            dma((n_hid - 1,)),
            dma((n_hid - 1,)),
        ],
        compiler_params=pltpu.CompilerParams(
            collective_id=0, has_side_effects=True, vmem_limit_bytes=60 * 1024 * 1024
        ),
        cost_estimate=pl.CostEstimate(
            flops=work, bytes_accessed=n_hid * experts * depth * units * 6, transcendentals=0
        ),
        name="expert_layer",
    )(tokens, expert_ids, gate_probs, gate_weight, up_weight, down_weight)


def solution(mesh):
    in_specs = (
        P(("grp", "hid"), "wid"),
        P("grp", None),
        P("grp", None),
        P(None, "wid", "hid"),
        P(None, "wid", "hid"),
        P(None, "hid", "wid"),
    )
    out_specs = P(("grp", "hid"), "wid")
    return jax.shard_map(
        functools.partial(shards, mesh.shape["wid"], mesh.shape["hid"]),
        mesh=mesh, in_specs=in_specs, out_specs=out_specs, check_vma=False,
    )
```
